32 devices in a mesh: island: 4 (over y, x), fsdp: 8 (over z, core).
Axes of the slice: x: 2, y: 2, z: 4, core: 2. Of those that a mesh axis runs over, the one named last changes fastest.
Arguments:
- weights: bfloat16 [4096, 14336], P(None, 'fsdp'), may hold values from -3 to 3
- momentum: bfloat16 [4096, 14336], P(None, 'fsdp'), may hold values from -0.59765625 to 0.59765625
- table: bfloat16 [2048, 4096], P(None, 'fsdp'), may hold values from -6 to 6
- token_ids: int32 [4, 2, 896], P('island'), may hold values from 0 to 2047
- cotangent: bfloat16 [4, 2, 896, 14336], P('island', None, None, 'fsdp'), may hold values from -6 to 6
Outputs:
- new_weights: bfloat16 [4096, 14336], P(None, 'fsdp')
The draws below stay inside these ranges and needn't reach their ends.
All inputs are finite; a program needn't handle non-finite values.
Results may differ from the reference program's by a relative error of at most 0.005.
Values may be sent and summed in bfloat16 or wider, within the bound.
A program may use at most 128 MiB of HBM per device.

```python
import math
import jax
import jax.numpy as jnp
from jax import lax

D = 4096
FF = 14336
TOK = 896
ROWS = 2048
STEPS = 2
ISLANDS = 4
N_ISLAND = 4


def touch_ends(values, own_key, low, largest):
    place = [jax.random.randint(jax.random.fold_in(own_key, axis), (), 0, length) for axis, length in enumerate(values.shape)]
    longest = values.shape.index(max(values.shape))
    next_to = place[:longest] + [(place[longest] + 1) % values.shape[longest]] + place[longest + 1:]
    return values.at[tuple(place)].set(low).at[tuple(next_to)].set(largest)


def block_scale(stream_key, extent, split, smallest, high):
    loudness = 1.0
    for position, parts in split:
        heights = jax.random.uniform(jax.random.fold_in(jax.random.fold_in(stream_key, 6), position), (parts,), jnp.float32, smallest / len(split), high / len(split))
        loudness = loudness * jnp.repeat(jnp.exp(heights), extent[position] // parts).reshape((-1,) + (1,) * (len(extent) - 1 - position))
    return loudness


def gaussian(key, shape, deviation, reach, shards=(), kind=jnp.bfloat16):
    loudness = block_scale(key, shape, shards, -0.22, 0.18) if shards else 1.0
    array = jax.random.normal(key, shape, jnp.float32) * deviation * loudness
    return jnp.minimum(jnp.maximum(array, -reach), reach).astype(kind)


def setup_inputs(seed: int = 0) -> dict:
    streams_of = jax.random.split(jax.random.key(seed), 6)
    weights = gaussian(streams_of[0], (D, FF), 0.5, 3.0, ((1, 8),))
    momentum = gaussian(streams_of[1], (D, FF), 0.1, 0.59765625, ((1, 8),))
    table = gaussian(streams_of[2], (ROWS, D), 1.0, 6.0, ((1, 8),))
    token_ids = touch_ends(jax.random.randint(streams_of[3], (ISLANDS, STEPS, TOK), 0, ROWS), jax.random.fold_in(streams_of[3], 1), 0, ROWS - 1).astype(jnp.int32)
    cotangent = gaussian(streams_of[4], (ISLANDS, STEPS, TOK, FF), 1.0, 6.0, ((0, 4), (3, 8)))
    return dict(weights=weights, momentum=momentum, table=table, token_ids=token_ids, cotangent=cotangent)


beta_one = 0.9
beta_two = 0.95
adam_eps = 0.0001
inner_rate = 0.1
decay_rate = 0.1
outer_rate = 0.7
outer_moment = 0.9

def silu_slope(hidden):
    sigma = jax.nn.sigmoid(hidden)
    return sigma * (1.0 + hidden * (1.0 - sigma))

def island_delta(weights, table, island_ids, island_cot):
    scale = 1.0 / math.sqrt(D)
    start = weights.astype(jnp.float32)
    local = start
    first = jnp.zeros((D, FF), jnp.float32)
    second = jnp.zeros((D, FF), jnp.float32)
    for step in range(STEPS):
        work = weights if step == 0 else local.astype(jnp.bfloat16)
        inputs = jnp.take(table, island_ids[step], axis=0)
        hidden = jnp.dot(inputs, work, preferred_element_type=jnp.float32) * scale
        upstream = (island_cot[step].astype(jnp.float32) * silu_slope(hidden) / TOK).astype(jnp.bfloat16)
        grad = jnp.dot(inputs.T, upstream, preferred_element_type=jnp.float32) * scale
        first = beta_one * first + (1.0 - beta_one) * grad
        second = beta_two * second + (1.0 - beta_two) * grad * grad
        m_hat = first / (1.0 - beta_one ** (step + 1))
        v_hat = second / (1.0 - beta_two ** (step + 1))
        local = local - inner_rate * (m_hat / (jnp.sqrt(v_hat) + adam_eps) + decay_rate * local)
    return (start - local).astype(jnp.bfloat16).astype(jnp.float32)

def reference(weights, momentum, table, token_ids, cotangent):

    def add_island(index, total):
        return total + island_delta(weights, table, token_ids[index], cotangent[index])
    total = lax.fori_loop(0, N_ISLAND, add_island, jnp.zeros((D, FF), jnp.float32))
    mean = total / N_ISLAND
    moment = outer_moment * momentum.astype(jnp.float32) + mean
    fresh = weights.astype(jnp.float32) - outer_rate * (mean + outer_moment * moment)
    return fresh.astype(jnp.bfloat16)
```

```python
import functools
import math

import jax
import jax.numpy as jnp
from jax import lax
from jax.experimental import pallas as pl
from jax.experimental.pallas import tpu as pltpu
from jax.sharding import PartitionSpec as P

beta_one = 0.9
beta_two = 0.95
adam_eps = 0.0001
inner_rate = 0.1
decay_rate = 0.1
outer_rate = 0.7
outer_moment = 0.9

CHUNKS = 8


def silu_slope(hidden):
    sigma = jax.nn.sigmoid(hidden)
    return sigma * (1.0 + hidden * (1.0 - sigma))


def first_move(grad):
    return grad / (jnp.abs(grad) + adam_eps)


def second_move(grad_one, grad_two):
    first = beta_one * (1.0 - beta_one) * grad_one + (1.0 - beta_one) * grad_two
    second = (
        beta_two * (1.0 - beta_two) * grad_one * grad_one
        + (1.0 - beta_two) * grad_two * grad_two
    )
    m_hat = first * (1.0 / (1.0 - beta_one**2))
    v_hat = second * (1.0 / (1.0 - beta_two**2))
    return m_hat / (jnp.sqrt(v_hat) + adam_eps)


def step_kernel(step, shape, side, ids, pieces, weights, *refs):
    tiles, tok, scale = shape
    if step == 0:
        cot_own, cot_other, out, picks, turned, hidden, upstream = refs
    else:
        grad_one, cot_own, cot_other, out, picks, turned, hidden, upstream = refs
    at = pl.program_id(0)
    feat = pieces.shape[-1]
    rows = picks.shape[1]
    keep = 1.0 - inner_rate * decay_rate

    @pl.when(at == 0)
    def _():
        hidden[...] = jnp.zeros_like(hidden)

        @pl.loop(0, 2 * tok // 128)
        def _(part):
            span = pl.ds(pl.multiple_of(part * 128, 128), 128)
            row = lax.broadcasted_iota(jnp.int32, (128, rows), 1)
            picks[span, :] = (row == ids[span, :]).astype(jnp.float32).astype(jnp.bfloat16)

    @pl.when(at < tiles)
    def _():
        table = pieces[...].reshape(rows, feat)
        base = weights[...]
        place = pl.ds(pl.multiple_of(at * feat, feat), feat)
        for island in range(2):
            span = pl.ds(island * tok, tok)
            chosen = jnp.dot(
                picks[span, :], table, preferred_element_type=jnp.float32
            ).astype(jnp.bfloat16)
            turned[place, span] = chosen.T
            if step == 0:
                work = base
            else:
                moved = first_move(grad_one[island].astype(jnp.float32))
                work = (keep * base.astype(jnp.float32) - inner_rate * moved).astype(jnp.bfloat16)
            hidden[span, :] += jnp.dot(chosen, work, preferred_element_type=jnp.float32)

    @pl.when(at == tiles - 1)
    def _():
        for island, cot in enumerate((cot_own, cot_other)):

            @pl.loop(0, tok // 128)
            def _(part):
                inner = pl.ds(pl.multiple_of(part * 128, 128), 128)
                span = pl.ds(pl.multiple_of(island * tok + part * 128, 128), 128)
                value = cot[inner, :].astype(jnp.float32) * silu_slope(hidden[span, :] * scale)
                upstream[span, :] = (value * (1.0 / tok)).astype(jnp.bfloat16)

    @pl.when(at >= tiles)
    def _():
        place = pl.ds(pl.multiple_of((at - tiles) * feat, feat), feat)
        grads = [
            jnp.dot(
                turned[place, pl.ds(island * tok, tok)],
                upstream[pl.ds(island * tok, tok), :],
                preferred_element_type=jnp.float32,
            )
            * scale
            for island in range(2)
        ]
        if step == 0:
            for island in range(2):
                out[island] = grads[island].astype(jnp.bfloat16)
        else:
            total = (2.0 * (1.0 - keep * keep)) * weights[...].astype(jnp.float32)
            for island in range(2):
                one = grad_one[island].astype(jnp.float32)
                total += (keep * inner_rate) * first_move(one)
                total += inner_rate * second_move(one, grads[island])
            out[...] = total.astype(jnp.bfloat16)


def take_half(array, which, half):
    return lax.dynamic_slice_in_dim(array, which * half, half, array.ndim - 1)


def inner_step(step, side, ids, pieces, weights, grad_one, cot, cot_other):
    groups, tiles, quarter, feat = pieces.shape
    tok, half = cot_other.shape[1:]
    depth = weights.shape[0]
    rows = groups * quarter
    narrow = weights.shape[1] == half
    column = (lambda side: 0) if narrow else (lambda side: side[0])
    scale = 1.0 / math.sqrt(depth)
    block = lambda at: jnp.where(at < tiles, at, at - tiles)
    late = lambda at: jnp.maximum(at - tiles, 0)
    in_specs = [
        pl.BlockSpec((2 * tok, 1), lambda at, side: (0, 0)),
        pl.BlockSpec(
            (groups, None, quarter, feat),
            lambda at, side: (0, jnp.minimum(at, tiles - 1), 0, 0),
        ),
    ]
    operands = [ids, pieces, weights]
    if step == 0:
        in_specs.append(
            pl.BlockSpec((feat, half), lambda at, side: (jnp.minimum(at, tiles - 1), column(side)))
        )
        out_shape = jax.ShapeDtypeStruct((2, depth, half), jnp.bfloat16)
        out_spec = pl.BlockSpec((2, feat, half), lambda at, side: (0, late(at), 0))
    else:
        in_specs.append(pl.BlockSpec((feat, half), lambda at, side: (block(at), column(side))))
        in_specs.append(pl.BlockSpec((2, feat, half), lambda at, side: (0, block(at), 0)))
        operands.append(grad_one)
        out_shape = jax.ShapeDtypeStruct((depth, half), jnp.bfloat16)
        out_spec = pl.BlockSpec((feat, half), lambda at, side: (late(at), 0))
    in_specs += [
        pl.BlockSpec((None, tok, half), lambda at, side: (step, 0, column(side))),
        pl.BlockSpec((None, tok, half), lambda at, side: (step, 0, 0)),
    ]
    operands += [cot, cot_other]
    return pl.pallas_call(
        functools.partial(step_kernel, step, (tiles, tok, scale)),
        grid_spec=pltpu.PrefetchScalarGridSpec(
            num_scalar_prefetch=1,
            grid=(2 * tiles,),
            in_specs=in_specs,
            out_specs=out_spec,
            scratch_shapes=[
                pltpu.VMEM((2 * tok, rows), jnp.bfloat16),
                pltpu.VMEM((depth, 2 * tok), jnp.bfloat16),
                pltpu.VMEM((2 * tok, half), jnp.float32),
                pltpu.VMEM((2 * tok, half), jnp.bfloat16),
            ],
        ),
        out_shape=out_shape,
        compiler_params=pltpu.CompilerParams(vmem_limit_bytes=60 * 1024 * 1024),
        cost_estimate=pl.CostEstimate(
            flops=2 * 2 * tok * depth * (rows + 2 * half),
            bytes_accessed=60_000_000,
            transcendentals=0,
        ),
        name=f"inner_step_{step}",
    )(side, *operands)


def sum_update_kernel(islands, side, own, other, weights, momentum, held, fresh, placed):
    total = own[...].astype(jnp.float32) + other[...].astype(jnp.float32)
    mean = total * (1.0 / islands)
    moment = outer_moment * momentum[...].astype(jnp.float32) + mean
    base = weights[...].astype(jnp.float32)
    value = (base - outer_rate * (mean + outer_moment * moment)).astype(jnp.bfloat16)
    fresh[...] = value
    placed[...] = value


def plain_update(islands, chunk, own, other, weights, momentum):
    size = own.shape[0]
    span = slice(chunk * size, (chunk + 1) * size)
    mean = (own.astype(jnp.float32) + other.astype(jnp.float32)) / islands
    moment = outer_moment * momentum[span].astype(jnp.float32) + mean
    base = weights[span].astype(jnp.float32)
    return (base - outer_rate * (mean + outer_moment * moment)).astype(jnp.bfloat16)


def outer_update(islands, chunk, side, own, other, weights, momentum, held):
    size, half = own.shape
    rows = size // 2 if size % 32 == 0 else size
    steps = size // rows
    local = pl.BlockSpec((rows, half), lambda at, side: (at, 0))
    wide = pl.BlockSpec((rows, half), lambda at, side: (chunk * steps + at, side[0]))
    return pl.pallas_call(
        functools.partial(sum_update_kernel, islands),
        grid_spec=pltpu.PrefetchScalarGridSpec(
            num_scalar_prefetch=1,
            grid=(steps,),
            in_specs=[local, local, wide, wide, pl.BlockSpec(memory_space=pl.ANY)],
            out_specs=[local, wide],
        ),
        out_shape=[
            jax.ShapeDtypeStruct(own.shape, jnp.bfloat16),
            jax.ShapeDtypeStruct(held.shape, held.dtype),
        ],
        input_output_aliases={5: 1},
        compiler_params=pltpu.CompilerParams(vmem_limit_bytes=24 * 1024 * 1024),
        cost_estimate=pl.CostEstimate(
            flops=8 * size * half, bytes_accessed=12 * size * half, transcendentals=0
        ),
        name=f"outer_update_{chunk}",
    )(side, own, other, weights, momentum, held)


def place_kernel(side, block, held, placed):
    placed[...] = block[...]


def place(chunk, side, block, held):
    size, half = block.shape
    return pl.pallas_call(
        place_kernel,
        grid_spec=pltpu.PrefetchScalarGridSpec(
            num_scalar_prefetch=1,
            grid=(1,),
            in_specs=[
                pl.BlockSpec((size, half), lambda at, side: (0, 0)),
                pl.BlockSpec(memory_space=pl.ANY),
            ],
            out_specs=pl.BlockSpec((size, half), lambda at, side: (chunk, 1 - side[0])),
        ),
        out_shape=jax.ShapeDtypeStruct(held.shape, held.dtype),
        input_output_aliases={2: 0},
        compiler_params=pltpu.CompilerParams(vmem_limit_bytes=24 * 1024 * 1024),
        cost_estimate=pl.CostEstimate(
            flops=0, bytes_accessed=4 * size * half, transcendentals=0
        ),
        name=f"place_{chunk}",
    )(side, block, held)


def body(weights, momentum, table, token_ids, cotangent):
    islands = lax.axis_size("island")
    shards = lax.axis_size("fsdp")
    me = lax.axis_index("island")
    depth, columns = weights.shape
    half = columns // 2
    rows, feat = table.shape
    quarter = rows // islands
    partner = [(i, i ^ 1) for i in range(islands)]
    side = lax.rem(me, 2).astype(jnp.int32).reshape(1)

    mine = lax.dynamic_slice_in_dim(table, me * quarter, quarter, 0)
    pieces = lax.all_gather(mine, ("island", "fsdp"), axis=0, tiled=False)
    pieces = pieces.reshape(islands, shards, quarter, feat)

    cot = cotangent[0]
    ids_other = lax.ppermute(token_ids[0], "island", partner)
    to_send = lax.dynamic_slice_in_dim(cot, (1 - side[0]) * half, half, 2)
    cot_other = lax.ppermute(to_send, "island", partner)
    ids = jnp.stack([token_ids[0], ids_other], axis=1)

    steps, tok = token_ids.shape[1:]
    aligned = half % 128 == 0
    if not aligned:
        cot, weights, momentum = (take_half(a, side[0], half) for a in (cot, weights, momentum))
    grad_one = inner_step(
        0, side, ids[0].reshape(2 * tok, 1), pieces, weights, None, cot, cot_other
    )
    part = inner_step(
        1, side, ids[1].reshape(2 * tok, 1), pieces, weights, grad_one, cot, cot_other
    )

    held = jnp.zeros(weights.shape, jnp.bfloat16) if aligned else None
    size = depth // CHUNKS
    fresh, kept = [], []
    for chunk in range(CHUNKS):
        own = lax.slice_in_dim(part, chunk * size, (chunk + 1) * size, axis=0)
        reach = 2
        while reach < islands:
            other = lax.ppermute(own, "island", [(i, i ^ reach) for i in range(islands)])
            if 2 * reach < islands:
                own = (own.astype(jnp.float32) + other.astype(jnp.float32)).astype(jnp.bfloat16)
            reach *= 2
        if aligned:
            mine, held = outer_update(islands, chunk, side, own, other, weights, momentum, held)
        else:
            mine = plain_update(islands, chunk, own, other, weights, momentum)
            kept.append(mine)
        fresh.append(lax.ppermute(mine, "island", partner))
    if not aligned:
        low = jnp.concatenate(kept, axis=0)
        high = jnp.concatenate(fresh, axis=0)
        first = side[0] == 0
        return jnp.concatenate(
            [jnp.where(first, low, high), jnp.where(first, high, low)], axis=1
        )
    for chunk in range(CHUNKS):
        held = place(chunk, side, fresh[chunk], held)
    return held


def solution(mesh):
    placed = (
        P(None, "fsdp"),
        P(None, "fsdp"),
        P(None, "fsdp"),
        P("island", None, None),
        P("island", None, None, "fsdp"),
    )
    return jax.shard_map(
        body, mesh=mesh, in_specs=placed, out_specs=P(None, "fsdp"), check_vma=False
    )
```

```python
import functools
import math

import jax
import jax.numpy as jnp
from jax import lax
from jax.experimental import pallas as pl
from jax.experimental.pallas import tpu as pltpu
from jax.sharding import PartitionSpec as P

beta_one = 0.9
beta_two = 0.95
adam_eps = 0.0001
inner_rate = 0.1
decay_rate = 0.1
outer_rate = 0.7
outer_moment = 0.9

CHUNKS = 8


def silu_slope(hidden):
    sigma = jax.nn.sigmoid(hidden)
    return sigma * (1.0 + hidden * (1.0 - sigma))


def first_move(grad):
    return grad / (jnp.abs(grad) + adam_eps)


def second_move(grad_one, grad_two):
    first = beta_one * (1.0 - beta_one) * grad_one + (1.0 - beta_one) * grad_two
    second = (
        beta_two * (1.0 - beta_two) * grad_one * grad_one
        + (1.0 - beta_two) * grad_two * grad_two
    )
    m_hat = first * (1.0 / (1.0 - beta_one**2))
    v_hat = second * (1.0 / (1.0 - beta_two**2))
    return m_hat / (jnp.sqrt(v_hat) + adam_eps)


def params(mib):
    return pltpu.CompilerParams(vmem_limit_bytes=mib * 1024 * 1024)


def pick_kernel(part, tok, side, ids, pieces, weights, *refs):
    early, late, hidden, picks = refs[-4:]
    rows, feat = picks.shape[1], pieces.shape[-1]

    @pl.when(pl.program_id(0) == 0)
    def _():
        hidden[...] = jnp.zeros_like(hidden) if part == 0 else refs[0][...]

        @pl.loop(0, 4 * tok // 128)
        def _(block):
            span = pl.ds(pl.multiple_of(block * 128, 128), 128)
            row = lax.broadcasted_iota(jnp.int32, (128, rows), 1)
            picks[span, :] = (row == ids[span, :]).astype(jnp.float32).astype(jnp.bfloat16)

    shard = pieces[...].reshape(rows, feat)
    for island in range(2):
        span = pl.ds(island * tok, tok)
        chosen = jnp.dot(picks[span, :], shard, preferred_element_type=jnp.float32)
        chosen = chosen.astype(jnp.bfloat16)
        early[island] = chosen.T
        hidden[span, :] += jnp.dot(chosen, weights[...], preferred_element_type=jnp.float32)
        chosen = jnp.dot(
            picks[pl.ds((2 + island) * tok, tok), :], shard, preferred_element_type=jnp.float32
        )
        late[island] = chosen.astype(jnp.bfloat16).T


def pick(part, parts, column, side, ids, pieces, weights, half, behind):
    groups, tiles, quarter, feat = pieces.shape
    tok = ids.shape[0] // 4
    whole = pl.BlockSpec((2 * tok, half), lambda at, side: (0, 0), pipeline_mode=pl.Buffered(1))
    in_specs = [
        pl.BlockSpec((4 * tok, 1), lambda at, side: (0, 0), pipeline_mode=pl.Buffered(1)),
        pl.BlockSpec((groups, None, quarter, feat), lambda at, side: (0, at, 0, 0)),
        pl.BlockSpec((feat, half), lambda at, side: (parts * at + part, column(side))),
    ]
    operands = [ids, pieces, weights]
    if part:
        in_specs += [whole] + [pl.BlockSpec(memory_space=pl.ANY)] * 2
        operands += behind
    return pl.pallas_call(
        functools.partial(pick_kernel, part, tok),
        grid_spec=pltpu.PrefetchScalarGridSpec(
            num_scalar_prefetch=1,
            grid=(tiles,),
            in_specs=in_specs,
            out_specs=[
                pl.BlockSpec((2, None, feat, tok), lambda at, side: (0, part, at, 0)),
                pl.BlockSpec((2, None, feat, tok), lambda at, side: (0, part, at, 0)),
                pl.BlockSpec((2 * tok, half), lambda at, side: (0, 0)),
            ],
            scratch_shapes=[pltpu.VMEM((4 * tok, groups * quarter), jnp.bfloat16)],
        ),
        out_shape=[
            jax.ShapeDtypeStruct((2, parts, tiles * feat, tok), jnp.bfloat16),
            jax.ShapeDtypeStruct((2, parts, tiles * feat, tok), jnp.bfloat16),
            jax.ShapeDtypeStruct((2 * tok, half), jnp.float32),
        ],
        input_output_aliases={4: 2, 5: 0, 6: 1} if part else {},
        compiler_params=params(56),
        cost_estimate=pl.CostEstimate(
            flops=2 * 2 * tok * tiles * feat * (2 * groups * quarter + half),
            bytes_accessed=50_000_000,
            transcendentals=0,
        ),
        name=f"pick_{part}",
    )(side, *operands)


def make_upstream(hidden, cots, scale, upstream):
    tok = cots[0].shape[0]
    for island, cot in enumerate(cots):

        @pl.loop(0, tok // 128)
        def _(part):
            inner = pl.ds(pl.multiple_of(part * 128, 128), 128)
            span = pl.ds(pl.multiple_of(island * tok + part * 128, 128), 128)
            value = cot[inner, :].astype(jnp.float32) * silu_slope(hidden[span, :] * scale)
            upstream[span, :] = (value * (1.0 / tok)).astype(jnp.bfloat16)


def middle_kernel(
    scale, side, hidden, own, other, own_late, other_late, early, late, weights,
    grad_one, upstream_late, upstream, hidden_late,
):
    tok = own.shape[0]
    parts, part = early.shape[1:3]
    keep = 1.0 - inner_rate * decay_rate
    at = pl.program_id(0)

    @pl.when(at == 0)
    def _():
        make_upstream(hidden, (own, other), scale, upstream)
        hidden_late[...] = jnp.zeros_like(hidden_late)

    @pl.loop(0, parts)
    def _(index):
        place = pl.ds(pl.multiple_of(index * part, part), part)
        base = weights[place, :].astype(jnp.float32)
        for island in range(2):
            span = pl.ds(island * tok, tok)
            grad = scale * jnp.dot(
                early[island, index], upstream[span, :], preferred_element_type=jnp.float32
            )
            grad_one[island, index] = grad.astype(jnp.bfloat16)
            work = (keep * base - inner_rate * first_move(grad)).astype(jnp.bfloat16)
            hidden_late[span, :] += jnp.dot(
                late[island, index].T, work, preferred_element_type=jnp.float32
            )

    @pl.when(at == pl.num_programs(0) - 1)
    def _():
        make_upstream(hidden_late, (own_late, other_late), scale, upstream_late)


def middle(tiles, column, side, hidden, cot, cot_other, early, late, weights):
    double, half = hidden.shape
    tok = double // 2
    depth = weights.shape[0]
    parts = early.shape[1]
    part = early.shape[2] // tiles
    once = pl.Buffered(1)
    cot_spec = lambda step, side_of: pl.BlockSpec(
        (None, tok, half), lambda at, side: (step, 0, side_of(side)), pipeline_mode=once
    )
    none = lambda side: 0
    tall = lambda width: pl.BlockSpec((2, parts, part, width), lambda at, side: (0, 0, at, 0))
    return pl.pallas_call(
        functools.partial(middle_kernel, 1.0 / math.sqrt(depth)),
        grid_spec=pltpu.PrefetchScalarGridSpec(
            num_scalar_prefetch=1,
            grid=(tiles,),
            in_specs=[
                pl.BlockSpec((double, half), lambda at, side: (0, 0), pipeline_mode=once),
                cot_spec(0, column),
                cot_spec(0, none),
                cot_spec(1, column),
                cot_spec(1, none),
                tall(tok),
                tall(tok),
                pl.BlockSpec((parts * part, half), lambda at, side: (at, column(side))),
            ],
            out_specs=[
                tall(half),
                pl.BlockSpec((double, half), lambda at, side: (0, 0)),
            ],
            scratch_shapes=[
                pltpu.VMEM((double, half), jnp.bfloat16),
                pltpu.VMEM((double, half), jnp.float32),
            ],
        ),
        out_shape=[
            jax.ShapeDtypeStruct(early.shape[:3] + (half,), jnp.bfloat16),
            jax.ShapeDtypeStruct((double, half), jnp.bfloat16),
        ],
        input_output_aliases={6: 0} if tok == half else {},
        compiler_params=params(60),
        cost_estimate=pl.CostEstimate(
            flops=2 * 2 * double * depth * half, bytes_accessed=90_000_000, transcendentals=0
        ),
        name="middle",
    )(side, hidden, cot, cot_other, cot, cot_other, early, late, weights)


def last_kernel(scale, side, late, upstream, grad_one, weights, *refs):
    out = refs[-1]
    tok = upstream.shape[0] // 2
    parts, part = late.shape[1:3]
    keep = 1.0 - inner_rate * decay_rate

    @pl.loop(0, parts * part // 128)
    def _(block):
        index, row = block // (part // 128), block % (part // 128)
        place = pl.ds(pl.multiple_of(block * 128, 128), 128)
        rows = pl.ds(pl.multiple_of(row * 128, 128), 128)
        total = (2.0 * (1.0 - keep * keep)) * weights[place, :].astype(jnp.float32)
        for island in range(2):
            span = pl.ds(island * tok, tok)
            grad = scale * jnp.dot(
                late[island, index, rows, :], upstream[span, :], preferred_element_type=jnp.float32
            )
            one = grad_one[island, index, rows, :].astype(jnp.float32)
            total += (keep * inner_rate) * first_move(one)
            total += inner_rate * second_move(one, grad)
        out[place, :] = total.astype(jnp.bfloat16)


def last(chunk, tiles, column, side, late, upstream, grad_one, weights, after):
    double, half = upstream.shape
    depth = weights.shape[0]
    size = depth // CHUNKS
    rows = depth // tiles
    steps = size // rows
    parts, tok = late.shape[1], late.shape[3]
    block = (2, parts, rows // parts)
    row = lambda at: chunk * steps + at
    return pl.pallas_call(
        functools.partial(last_kernel, 1.0 / math.sqrt(depth)),
        grid_spec=pltpu.PrefetchScalarGridSpec(
            num_scalar_prefetch=1,
            grid=(steps,),
            in_specs=[
                pl.BlockSpec(block + (tok,), lambda at, side: (0, 0, row(at), 0)),
                pl.BlockSpec((double, half), lambda at, side: (0, 0)),
                pl.BlockSpec(block + (half,), lambda at, side: (0, 0, row(at), 0)),
                pl.BlockSpec((rows, half), lambda at, side: (row(at), column(side))),
            ]
            + [pl.BlockSpec(memory_space=pl.ANY)] * len(after),
            out_specs=pl.BlockSpec((rows, half), lambda at, side: (at, 0)),
        ),
        out_shape=jax.ShapeDtypeStruct((size, half), jnp.bfloat16),
        compiler_params=params(60),
        cost_estimate=pl.CostEstimate(
            flops=2 * double * size * half, bytes_accessed=10_000_000, transcendentals=0
        ),
        name=f"last_{chunk}",
    )(side, late, upstream, grad_one, weights, *after)


def take_half(array, which, half):
    return lax.dynamic_slice_in_dim(array, which * half, half, array.ndim - 1)


def plain_update(islands, chunk, own, other, weights, momentum):
    size = own.shape[0]
    span = slice(chunk * size, (chunk + 1) * size)
    mean = (own.astype(jnp.float32) + other.astype(jnp.float32)) / islands
    moment = outer_moment * momentum[span].astype(jnp.float32) + mean
    base = weights[span].astype(jnp.float32)
    return (base - outer_rate * (mean + outer_moment * moment)).astype(jnp.bfloat16)


def sum_update_kernel(islands, side, own, other, weights, momentum, *refs):
    fresh, placed = refs[-2:]
    total = own[...].astype(jnp.float32) + other[...].astype(jnp.float32)
    mean = total * (1.0 / islands)
    moment = outer_moment * momentum[...].astype(jnp.float32) + mean
    base = weights[...].astype(jnp.float32)
    value = (base - outer_rate * (mean + outer_moment * moment)).astype(jnp.bfloat16)
    fresh[...] = value
    placed[...] = value


def outer_update(islands, chunk, side, own, other, weights, momentum, held):
    size, half = own.shape
    rows = size // 2 if size % 32 == 0 else size
    steps = size // rows
    behind = [] if held is None else [held]
    local = pl.BlockSpec((rows, half), lambda at, side: (at, 0))
    wide = pl.BlockSpec((rows, half), lambda at, side: (chunk * steps + at, side[0]))
    return pl.pallas_call(
        functools.partial(sum_update_kernel, islands),
        grid_spec=pltpu.PrefetchScalarGridSpec(
            num_scalar_prefetch=1,
            grid=(steps,),
            in_specs=[local, local, wide, wide]
            + [pl.BlockSpec(memory_space=pl.ANY)] * len(behind),
            out_specs=[local, wide],
        ),
        out_shape=[
            jax.ShapeDtypeStruct(own.shape, jnp.bfloat16),
            jax.ShapeDtypeStruct(weights.shape, weights.dtype),
        ],
        input_output_aliases={5: 1} if behind else {},
        compiler_params=params(60),
        cost_estimate=pl.CostEstimate(
            flops=8 * size * half, bytes_accessed=12 * size * half, transcendentals=0
        ),
        name=f"outer_update_{chunk}",
    )(side, own, other, weights, momentum, *behind)


def place_kernel(side, block, held, placed):
    placed[...] = block[...]


def place(chunk, side, block, held):
    size, half = block.shape
    return pl.pallas_call(
        place_kernel,
        grid_spec=pltpu.PrefetchScalarGridSpec(
            num_scalar_prefetch=1,
            grid=(1,),
            in_specs=[
                pl.BlockSpec((size, half), lambda at, side: (0, 0)),
                pl.BlockSpec(memory_space=pl.ANY),
            ],
            out_specs=pl.BlockSpec((size, half), lambda at, side: (chunk, 1 - side[0])),
        ),
        out_shape=jax.ShapeDtypeStruct(held.shape, held.dtype),
        input_output_aliases={2: 0},
        compiler_params=params(60),
        cost_estimate=pl.CostEstimate(
            flops=0, bytes_accessed=4 * size * half, transcendentals=0
        ),
        name=f"place_{chunk}",
    )(side, block, held)


def body(weights, momentum, table, token_ids, cotangent):
    islands = lax.axis_size("island")
    shards = lax.axis_size("fsdp")
    me = lax.axis_index("island")
    depth, columns = weights.shape
    half = columns // 2
    rows, feat = table.shape
    quarter = rows // islands
    partner = [(i, i ^ 1) for i in range(islands)]
    side = lax.rem(me, 2).astype(jnp.int32).reshape(1)

    parts = 2
    mine = lax.dynamic_slice_in_dim(table, me * quarter, quarter, 0)
    pieces = []
    for part in range(parts):
        cut = lax.slice_in_dim(mine, part * feat // parts, (part + 1) * feat // parts, axis=1)
        got = lax.all_gather(cut, ("island", "fsdp"), axis=0, tiled=False)
        pieces.append(got.reshape(islands, shards, quarter, feat // parts))

    cot = cotangent[0]
    ids_other = lax.ppermute(token_ids[0], "island", partner)
    to_send = lax.dynamic_slice_in_dim(cot, (1 - side[0]) * half, half, 2)
    cot_other = lax.ppermute(to_send, "island", partner)
    ids = jnp.stack([token_ids[0], ids_other], axis=1)

    steps, tok = token_ids.shape[1:]
    aligned = half % 128 == 0
    if not aligned:
        cot, weights, momentum = (take_half(a, side[0], half) for a in (cot, weights, momentum))
    column = (lambda side: side[0]) if aligned else (lambda side: 0)
    ids = ids.reshape(2 * steps * tok, 1)
    behind = []
    for part in range(parts):
        early, late, hidden = pick(
            part, parts, column, side, ids, pieces[part], weights, half, behind
        )
        behind = [hidden, early, late]
    grad_one, upstream = middle(
        shards, column, side, hidden, cot, cot_other, early, late, weights
    )

    held = None
    size = depth // CHUNKS
    fresh, kept, arrived = [], [], []
    for chunk in range(CHUNKS):
        after = [a[chunk - n] for a, n in ((arrived, 2), (fresh, 3)) if chunk >= n]
        own = last(chunk, shards, column, side, late, upstream, grad_one, weights, after)
        reach = 2
        while reach < islands:
            other = lax.ppermute(own, "island", [(i, i ^ reach) for i in range(islands)])
            if 2 * reach < islands:
                own = (own.astype(jnp.float32) + other.astype(jnp.float32)).astype(jnp.bfloat16)
            reach *= 2
        arrived.append(other)
        if aligned:
            mine, held = outer_update(islands, chunk, side, own, other, weights, momentum, held)
        else:
            mine = plain_update(islands, chunk, own, other, weights, momentum)
            kept.append(mine)
        fresh.append(lax.ppermute(mine, "island", partner))
    if not aligned:
        low = jnp.concatenate(kept, axis=0)
        high = jnp.concatenate(fresh, axis=0)
        first = side[0] == 0
        return jnp.concatenate(
            [jnp.where(first, low, high), jnp.where(first, high, low)], axis=1
        )
    for chunk in range(CHUNKS):
        held = place(chunk, side, fresh[chunk], held)
    return held


def solution(mesh):
    placed = (
        P(None, "fsdp"),
        P(None, "fsdp"),
        P(None, "fsdp"),
        P("island", None, None),
        P("island", None, None, "fsdp"),
    )
    return jax.shard_map(
        body, mesh=mesh, in_specs=placed, out_specs=P(None, "fsdp"), check_vma=False
    )
```

```python
import functools
import math

import jax
import jax.numpy as jnp
from jax import lax
from jax.experimental import pallas as pl
from jax.experimental.pallas import tpu as pltpu
from jax.sharding import PartitionSpec as P

beta_one = 0.9
beta_two = 0.95
adam_eps = 0.0001
inner_rate = 0.1
decay_rate = 0.1
outer_rate = 0.7
outer_moment = 0.9

CHUNKS = 8


def silu_slope(hidden):
    sigma = jax.nn.sigmoid(hidden)
    return sigma * (1.0 + hidden * (1.0 - sigma))


def first_move(grad):
    return grad / (jnp.abs(grad) + adam_eps)


def second_move(grad_one, grad_two):
    first = beta_one * (1.0 - beta_one) * grad_one + (1.0 - beta_one) * grad_two
    second = (
        beta_two * (1.0 - beta_two) * grad_one * grad_one
        + (1.0 - beta_two) * grad_two * grad_two
    )
    m_hat = first * (1.0 / (1.0 - beta_one**2))
    v_hat = second * (1.0 / (1.0 - beta_two**2))
    return m_hat / (jnp.sqrt(v_hat) + adam_eps)


def params(mib):
    return pltpu.CompilerParams(vmem_limit_bytes=mib * 1024 * 1024)


def pick_kernel(part, tok, side, ids, pieces, weights, *refs):
    early, late, hidden, picks = refs[-4:]
    rows, feat = picks.shape[1], pieces.shape[-1]

    @pl.when(pl.program_id(0) == 0)
    def _():
        hidden[...] = jnp.zeros_like(hidden) if part == 0 else refs[0][...]

        @pl.loop(0, 4 * tok // 128)
        def _(block):
            span = pl.ds(pl.multiple_of(block * 128, 128), 128)
            row = lax.broadcasted_iota(jnp.int32, (128, rows), 1)
            picks[span, :] = (row == ids[span, :]).astype(jnp.float32).astype(jnp.bfloat16)

    shard = pieces[...].reshape(rows, feat)
    for island in range(2):
        span = pl.ds(island * tok, tok)
        chosen = jnp.dot(picks[span, :], shard, preferred_element_type=jnp.float32)
        chosen = chosen.astype(jnp.bfloat16)
        early[island] = chosen.T
        hidden[span, :] += jnp.dot(chosen, weights[...], preferred_element_type=jnp.float32)
        chosen = jnp.dot(
            picks[pl.ds((2 + island) * tok, tok), :], shard, preferred_element_type=jnp.float32
        )
        late[island] = chosen.astype(jnp.bfloat16).T


def pick(part, parts, column, side, ids, pieces, weights, half, behind):
    groups, tiles, quarter, feat = pieces.shape
    tok = ids.shape[0] // 4
    whole = pl.BlockSpec((2 * tok, half), lambda at, side: (0, 0), pipeline_mode=pl.Buffered(1))
    in_specs = [
        pl.BlockSpec((4 * tok, 1), lambda at, side: (0, 0), pipeline_mode=pl.Buffered(1)),
        pl.BlockSpec((groups, None, quarter, feat), lambda at, side: (0, at, 0, 0)),
        pl.BlockSpec((feat, half), lambda at, side: (parts * at + part, column(side))),
    ]
    operands = [ids, pieces, weights]
    if part:
        in_specs += [whole] + [pl.BlockSpec(memory_space=pl.ANY)] * 2
        operands += behind
    return pl.pallas_call(
        functools.partial(pick_kernel, part, tok),
        grid_spec=pltpu.PrefetchScalarGridSpec(
            num_scalar_prefetch=1,
            grid=(tiles,),
            in_specs=in_specs,
            out_specs=[
                pl.BlockSpec((2, None, feat, tok), lambda at, side: (0, part, at, 0)),
                pl.BlockSpec((2, None, feat, tok), lambda at, side: (0, part, at, 0)),
                pl.BlockSpec((2 * tok, half), lambda at, side: (0, 0)),
            ],
            scratch_shapes=[pltpu.VMEM((4 * tok, groups * quarter), jnp.bfloat16)],
        ),
        out_shape=[
            jax.ShapeDtypeStruct((2, parts, tiles * feat, tok), jnp.bfloat16),
            jax.ShapeDtypeStruct((2, parts, tiles * feat, tok), jnp.bfloat16),
            jax.ShapeDtypeStruct((2 * tok, half), jnp.float32),
        ],
        input_output_aliases={4: 2, 5: 0, 6: 1} if part else {},
        compiler_params=params(56),
        cost_estimate=pl.CostEstimate(
            flops=2 * 2 * tok * tiles * feat * (2 * groups * quarter + half),
            bytes_accessed=50_000_000,
            transcendentals=0,
        ),
        name=f"pick_{part}",
    )(side, *operands)


def make_upstream(hidden, cots, scale, upstream):
    tok = cots[0].shape[0]
    for island, cot in enumerate(cots):

        @pl.loop(0, tok // 128)
        def _(part):
            inner = pl.ds(pl.multiple_of(part * 128, 128), 128)
            span = pl.ds(pl.multiple_of(island * tok + part * 128, 128), 128)
            value = cot[inner, :].astype(jnp.float32) * silu_slope(hidden[span, :] * scale)
            upstream[span, :] = (value * (1.0 / tok)).astype(jnp.bfloat16)


def middle_kernel(
    scale, side, hidden, own, other, early, late, weights, grad_one, hidden_late, upstream
):
    tok = own.shape[0]
    parts, part = early.shape[1:3]
    keep = 1.0 - inner_rate * decay_rate
    at = pl.program_id(0)

    @pl.when(at == 0)
    def _():
        make_upstream(hidden, (own, other), scale, upstream)
        hidden_late[...] = jnp.zeros_like(hidden_late)

    @pl.loop(0, parts)
    def _(index):
        place = pl.ds(pl.multiple_of(index * part, part), part)
        base = weights[place, :].astype(jnp.float32)
        for island in range(2):
            span = pl.ds(island * tok, tok)
            grad = scale * jnp.dot(
                early[island, index], upstream[span, :], preferred_element_type=jnp.float32
            )
            grad_one[island, index] = grad.astype(jnp.bfloat16)
            work = (keep * base - inner_rate * first_move(grad)).astype(jnp.bfloat16)
            hidden_late[span, :] += jnp.dot(
                late[island, index].T, work, preferred_element_type=jnp.float32
            )


def middle(tiles, column, side, hidden, cot, cot_other, early, late, weights):
    double, half = hidden.shape
    tok = double // 2
    depth = weights.shape[0]
    parts = early.shape[1]
    part = early.shape[2] // tiles
    once = pl.Buffered(1)
    tall = lambda width: pl.BlockSpec((2, parts, part, width), lambda at, side: (0, 0, at, 0))
    return pl.pallas_call(
        functools.partial(middle_kernel, 1.0 / math.sqrt(depth)),
        grid_spec=pltpu.PrefetchScalarGridSpec(
            num_scalar_prefetch=1,
            grid=(tiles,),
            in_specs=[
                pl.BlockSpec((double, half), lambda at, side: (0, 0), pipeline_mode=once),
                pl.BlockSpec(
                    (None, tok, half), lambda at, side: (0, 0, column(side)), pipeline_mode=once
                ),
                pl.BlockSpec((tok, half), lambda at, side: (0, 0), pipeline_mode=once),
                tall(tok),
                tall(tok),
                pl.BlockSpec((parts * part, half), lambda at, side: (at, column(side))),
            ],
            out_specs=[
                tall(half),
                pl.BlockSpec((double, half), lambda at, side: (0, 0)),
            ],
            scratch_shapes=[
                pltpu.VMEM((double, half), jnp.bfloat16),
            ],
        ),
        out_shape=[
            jax.ShapeDtypeStruct(early.shape[:3] + (half,), jnp.bfloat16),
            jax.ShapeDtypeStruct((double, half), jnp.float32),
        ],
        input_output_aliases={4: 0} if tok == half else {},
        compiler_params=params(60),
        cost_estimate=pl.CostEstimate(
            flops=2 * 2 * double * depth * half, bytes_accessed=90_000_000, transcendentals=0
        ),
        name="middle",
    )(side, hidden, cot, cot_other, early, late, weights)


def upstream_kernel(scale, side, hidden, own, other, upstream):
    make_upstream(hidden, (own, other), scale, upstream)


def upstream_of(step, depth, column, side, hidden, cot, cot_other):
    double, half = hidden.shape
    tok = double // 2
    whole = lambda shape: pl.BlockSpec(shape, lambda at, side: (0, 0))
    return pl.pallas_call(
        functools.partial(upstream_kernel, 1.0 / math.sqrt(depth)),
        grid_spec=pltpu.PrefetchScalarGridSpec(
            num_scalar_prefetch=1,
            grid=(1,),
            in_specs=[
                whole((double, half)),
                pl.BlockSpec((None, tok, half), lambda at, side: (step, 0, column(side))),
                whole((tok, half)),
            ],
            out_specs=whole((double, half)),
        ),
        out_shape=jax.ShapeDtypeStruct((double, half), jnp.bfloat16),
        compiler_params=params(60),
        cost_estimate=pl.CostEstimate(
            flops=30 * double * half, bytes_accessed=10 * double * half, transcendentals=0
        ),
        name="upstream",
    )(side, hidden, cot, cot_other)


def cut_kernel(side, cot, after, out):
    out[...] = cot[...]


def cut(step, side, cot, after):
    tok, columns = cot.shape[1:]
    half = columns // 2
    return pl.pallas_call(
        cut_kernel,
        grid_spec=pltpu.PrefetchScalarGridSpec(
            num_scalar_prefetch=1,
            grid=(2,),
            in_specs=[
                pl.BlockSpec((None, tok // 2, half), lambda at, side: (step, at, 1 - side[0])),
                pl.BlockSpec(memory_space=pl.ANY),
            ],
            out_specs=pl.BlockSpec((tok // 2, half), lambda at, side: (at, 0)),
        ),
        out_shape=jax.ShapeDtypeStruct((tok, half), cot.dtype),
        compiler_params=params(60),
        cost_estimate=pl.CostEstimate(
            flops=0, bytes_accessed=4 * tok * half, transcendentals=0
        ),
        name=f"cut_{step}",
    )(side, cot, after)


def last_kernel(scale, side, late, upstream, grad_one, weights, *refs):
    out = refs[-1]
    tok = upstream.shape[0] // 2
    parts, part = late.shape[1:3]
    keep = 1.0 - inner_rate * decay_rate

    @pl.loop(0, parts * part // 128)
    def _(block):
        index, row = block // (part // 128), block % (part // 128)
        place = pl.ds(pl.multiple_of(block * 128, 128), 128)
        rows = pl.ds(pl.multiple_of(row * 128, 128), 128)
        total = (2.0 * (1.0 - keep * keep)) * weights[place, :].astype(jnp.float32)
        for island in range(2):
            span = pl.ds(island * tok, tok)
            grad = scale * jnp.dot(
                late[island, index, rows, :], upstream[span, :], preferred_element_type=jnp.float32
            )
            one = grad_one[island, index, rows, :].astype(jnp.float32)
            total += (keep * inner_rate) * first_move(one)
            total += inner_rate * second_move(one, grad)
        out[place, :] = total.astype(jnp.bfloat16)


def last(chunk, tiles, column, side, late, upstream, grad_one, weights, after):
    double, half = upstream.shape
    depth = weights.shape[0]
    size = depth // CHUNKS
    rows = depth // tiles
    steps = size // rows
    parts, tok = late.shape[1], late.shape[3]
    block = (2, parts, rows // parts)
    row = lambda at: chunk * steps + at
    return pl.pallas_call(
        functools.partial(last_kernel, 1.0 / math.sqrt(depth)),
        grid_spec=pltpu.PrefetchScalarGridSpec(
            num_scalar_prefetch=1,
            grid=(steps,),
            in_specs=[
                pl.BlockSpec(block + (tok,), lambda at, side: (0, 0, row(at), 0)),
                pl.BlockSpec((double, half), lambda at, side: (0, 0)),
                pl.BlockSpec(block + (half,), lambda at, side: (0, 0, row(at), 0)),
                pl.BlockSpec((rows, half), lambda at, side: (row(at), column(side))),
            ]
            + [pl.BlockSpec(memory_space=pl.ANY)] * len(after),
            out_specs=pl.BlockSpec((rows, half), lambda at, side: (at, 0)),
        ),
        out_shape=jax.ShapeDtypeStruct((size, half), jnp.bfloat16),
        compiler_params=params(60),
        cost_estimate=pl.CostEstimate(
            flops=2 * double * size * half, bytes_accessed=10_000_000, transcendentals=0
        ),
        name=f"last_{chunk}",
    )(side, late, upstream, grad_one, weights, *after)


def take_half(array, which, half):
    return lax.dynamic_slice_in_dim(array, which * half, half, array.ndim - 1)


def plain_update(islands, chunk, own, other, weights, momentum):
    size = own.shape[0]
    span = slice(chunk * size, (chunk + 1) * size)
    mean = (own.astype(jnp.float32) + other.astype(jnp.float32)) / islands
    moment = outer_moment * momentum[span].astype(jnp.float32) + mean
    base = weights[span].astype(jnp.float32)
    return (base - outer_rate * (mean + outer_moment * moment)).astype(jnp.bfloat16)


def sum_update_kernel(islands, side, own, other, weights, momentum, *refs):
    fresh, placed = refs[-2:]
    total = own[...].astype(jnp.float32) + other[...].astype(jnp.float32)
    mean = total * (1.0 / islands)
    moment = outer_moment * momentum[...].astype(jnp.float32) + mean
    base = weights[...].astype(jnp.float32)
    value = (base - outer_rate * (mean + outer_moment * moment)).astype(jnp.bfloat16)
    fresh[...] = value
    placed[...] = value


def outer_update(islands, chunk, side, own, other, weights, momentum, held):
    size, half = own.shape
    rows = size // 2 if size % 32 == 0 else size
    steps = size // rows
    behind = [] if held is None else [held]
    local = pl.BlockSpec((rows, half), lambda at, side: (at, 0))
    wide = pl.BlockSpec((rows, half), lambda at, side: (chunk * steps + at, side[0]))
    return pl.pallas_call(
        functools.partial(sum_update_kernel, islands),
        grid_spec=pltpu.PrefetchScalarGridSpec(
            num_scalar_prefetch=1,
            grid=(steps,),
            in_specs=[local, local, wide, wide]
            + [pl.BlockSpec(memory_space=pl.ANY)] * len(behind),
            out_specs=[local, wide],
        ),
        out_shape=[
            jax.ShapeDtypeStruct(own.shape, jnp.bfloat16),
            jax.ShapeDtypeStruct(weights.shape, weights.dtype),
        ],
        input_output_aliases={5: 1} if behind else {},
        compiler_params=params(60),
        cost_estimate=pl.CostEstimate(
            flops=8 * size * half, bytes_accessed=12 * size * half, transcendentals=0
        ),
        name=f"outer_update_{chunk}",
    )(side, own, other, weights, momentum, *behind)


def place_kernel(side, block, held, placed):
    placed[...] = block[...]


def place(chunk, side, block, held):
    size, half = block.shape
    return pl.pallas_call(
        place_kernel,
        grid_spec=pltpu.PrefetchScalarGridSpec(
            num_scalar_prefetch=1,
            grid=(1,),
            in_specs=[
                pl.BlockSpec((size, half), lambda at, side: (0, 0)),
                pl.BlockSpec(memory_space=pl.ANY),
            ],
            out_specs=pl.BlockSpec((size, half), lambda at, side: (chunk, 1 - side[0])),
        ),
        out_shape=jax.ShapeDtypeStruct(held.shape, held.dtype),
        input_output_aliases={2: 0},
        compiler_params=params(60),
        cost_estimate=pl.CostEstimate(
            flops=0, bytes_accessed=4 * size * half, transcendentals=0
        ),
        name=f"place_{chunk}",
    )(side, block, held)


def body(weights, momentum, table, token_ids, cotangent):
    islands = lax.axis_size("island")
    shards = lax.axis_size("fsdp")
    me = lax.axis_index("island")
    depth, columns = weights.shape
    half = columns // 2
    rows, feat = table.shape
    quarter = rows // islands
    partner = [(i, i ^ 1) for i in range(islands)]
    side = lax.rem(me, 2).astype(jnp.int32).reshape(1)

    parts = 2
    mine = lax.dynamic_slice_in_dim(table, me * quarter, quarter, 0)
    pieces = []
    for part in range(parts):
        share = lax.slice_in_dim(mine, part * feat // parts, (part + 1) * feat // parts, axis=1)
        got = lax.all_gather(share, ("island", "fsdp"), axis=0, tiled=False)
        pieces.append(got.reshape(islands, shards, quarter, feat // parts))

    cot = cotangent[0]
    ids_other = lax.ppermute(token_ids[0], "island", partner)
    ids = jnp.stack([token_ids[0], ids_other], axis=1)

    steps, tok = token_ids.shape[1:]
    aligned = half % 128 == 0
    whole_cot = cot

    def partners(step, after):
        if aligned:
            sent = cut(step, side, whole_cot, after)
        else:
            sent = take_half(whole_cot[step], 1 - side[0], half)
        return lax.ppermute(sent, "island", partner)

    if not aligned:
        cot, weights, momentum = (take_half(a, side[0], half) for a in (cot, weights, momentum))
    column = (lambda side: side[0]) if aligned else (lambda side: 0)
    ids = ids.reshape(2 * steps * tok, 1)
    behind, cot_other = [], []
    for part in range(parts):
        early, late, hidden = pick(
            part, parts, column, side, ids, pieces[part], weights, half, behind
        )
        behind = [hidden, early, late]
        cot_other.append(partners(part, hidden))
    grad_one, hidden_late = middle(
        shards, column, side, hidden, cot, cot_other[0], early, late, weights
    )
    upstream = upstream_of(1, depth, column, side, hidden_late, cot, cot_other[1])

    held = None
    size = depth // CHUNKS
    fresh, kept, arrived = [], [], []
    for chunk in range(CHUNKS):
        after = [a[chunk - n] for a, n in ((arrived, 2), (fresh, 3)) if chunk >= n]
        own = last(chunk, shards, column, side, late, upstream, grad_one, weights, after)
        reach = 2
        while reach < islands:
            other = lax.ppermute(own, "island", [(i, i ^ reach) for i in range(islands)])
            if 2 * reach < islands:
                own = (own.astype(jnp.float32) + other.astype(jnp.float32)).astype(jnp.bfloat16)
            reach *= 2
        arrived.append(other)
        if aligned:
            mine, held = outer_update(islands, chunk, side, own, other, weights, momentum, held)
        else:
            mine = plain_update(islands, chunk, own, other, weights, momentum)
            kept.append(mine)
        fresh.append(lax.ppermute(mine, "island", partner))
    if not aligned:
        low = jnp.concatenate(kept, axis=0)
        high = jnp.concatenate(fresh, axis=0)
        first = side[0] == 0
        return jnp.concatenate(
            [jnp.where(first, low, high), jnp.where(first, high, low)], axis=1
        )
    for chunk in range(CHUNKS):
        held = place(chunk, side, fresh[chunk], held)
    return held


def solution(mesh):
    placed = (
        P(None, "fsdp"),
        P(None, "fsdp"),
        P(None, "fsdp"),
        P("island", None, None),
        P("island", None, None, "fsdp"),
    )
    return jax.shard_map(
        body, mesh=mesh, in_specs=placed, out_specs=P(None, "fsdp"), check_vma=False
    )
```
